32 devices in a mesh: span: 8 (over z, x), chord: 4 (over y, core).
Axes of the slice: x: 2, y: 2, z: 4, core: 2. Of those that a mesh axis runs over, the one named last changes fastest.
Arguments:
- displacement: bfloat16 [8, 4, 1024, 128], P('span', 'chord'), may hold values from -12 to 12
- packed_blocks: bfloat16 [8, 4, 1024, 1024], P('span', 'chord'), as said below
- flex_scale: float32 [8, 4, 1024], P('span', 'chord'), may hold values from 0.5 to 2
- dirichlet_scale: float32 [8, 4, 1024], P('span', 'chord'), may hold values from 0.5 to 2
- dirichlet_diag: bfloat16 [8, 4, 1024], P('span', 'chord'), may hold values from 1.1953125 to 2.5
- link_rows: int32 [8, 4, 4, 256], P('span', 'chord'), may hold values from 0 to 1023, as said below
- link_signs: int32 [8, 4, 4, 256], P('span', 'chord'), may hold values from -1 to 1, as said below
- link_counts: int32 [8, 4, 4], P('span', 'chord'), may hold values from 0 to 256, as said below
Outputs:
- multipliers: float32 [8, 4, 1024, 128], P('span', 'chord')
- residual: float32 [8, 4, 1024, 128], P('span', 'chord')
The draws below stay inside these ranges and needn't reach their ends.
Inputs may be any that keep to these rules, and one draw needn't show every extreme that they name: `link_rows`: for each subdomain the 4 x 256 entries name every row 0 to 1023 exactly once. `link_counts`: each count equals the count of the opposite direction on the neighbour's side; it is 0 at the edges of the mesh and toward unlisted neighbours, otherwise at least 64; some subdomain uses all 256 slots toward a span neighbour and some toward a chord neighbour. `link_signs`: every entry is 1 or -1; slot p toward a neighbour holds the opposite sign of slot p of the opposite direction on that neighbour. `packed_blocks`: each block's diagonal lies between 1.2 and 2.5.
All inputs are finite; a program needn't handle non-finite values.
Results may differ from the reference program's by a relative error of at most 0.0065.
Values may be sent and summed in bfloat16 or wider, within the bound.
A program may use at most 64 MiB of HBM per device.

```python
import math
import jax
import jax.numpy as jnp
from jax import lax

SUBS_SPAN = 8
SUBS_CHORD = 4
ROWS = 1024
LOADS = 128
SLOTS = 256
ITERS = 1


def link_tables(key):
    base = jax.random.fold_in(key, 4242)
    keys = jax.random.split(base, 7)
    shape2 = (SUBS_SPAN, SUBS_CHORD)
    span_ids = jnp.arange(SUBS_SPAN)[:, None]
    chord_ids = jnp.arange(SUBS_CHORD)[None, :]
    span_count = jax.random.randint(keys[0], shape2, SLOTS // 4, SLOTS + 1)
    span_count = jnp.where(jax.random.randint(keys[1], shape2, 0, 8) > 0, span_count, 0)
    span_count = span_count.at[0, 0].set(SLOTS)
    span_count = jnp.where(span_ids < SUBS_SPAN - 1, span_count, 0)
    chord_count = jax.random.randint(keys[2], shape2, SLOTS // 4, SLOTS + 1)
    chord_count = jnp.where(jax.random.randint(keys[3], shape2, 0, 8) > 0, chord_count, 0)
    chord_count = chord_count.at[0, 0].set(SLOTS)
    chord_count = jnp.where(chord_ids < SUBS_CHORD - 1, chord_count, 0)
    lower_span = jnp.concatenate([jnp.zeros((1, SUBS_CHORD), span_count.dtype), span_count[:-1]], axis=0)
    lower_chord = jnp.concatenate([jnp.zeros((SUBS_SPAN, 1), chord_count.dtype), chord_count[:, :-1]], axis=1)
    counts = jnp.stack([lower_span, span_count, lower_chord, chord_count], axis=-1).astype(jnp.int32)
    perm_keys = jax.random.split(keys[4], SUBS_SPAN * SUBS_CHORD)
    rows = jax.vmap(lambda k: jax.random.permutation(k, ROWS))(perm_keys)
    rows = rows.reshape(SUBS_SPAN, SUBS_CHORD, 4, SLOTS).astype(jnp.int32)
    span_sign = 2 * jax.random.randint(keys[5], (SUBS_SPAN, SUBS_CHORD, SLOTS), 0, 2) - 1
    chord_sign = 2 * jax.random.randint(keys[6], (SUBS_SPAN, SUBS_CHORD, SLOTS), 0, 2) - 1
    lower_span_sign = -jnp.roll(span_sign, 1, axis=0)
    lower_chord_sign = -jnp.roll(chord_sign, 1, axis=1)
    signs = jnp.stack([lower_span_sign, span_sign, lower_chord_sign, chord_sign], axis=2).astype(jnp.int32)
    return (rows, signs, counts)


def draw_link_rows(key, part):
    return link_tables(key)[0]


def draw_link_signs(key, part):
    return link_tables(key)[1]


def draw_link_counts(key, part):
    return link_tables(key)[2]


def draw_packed_blocks(key, part):
    keys = jax.random.split(jax.random.fold_in(key, 17), 2)
    shape = (SUBS_SPAN, SUBS_CHORD, ROWS, ROWS)
    spread = 0.4 / math.sqrt(ROWS)
    off = jax.random.normal(keys[0], shape, jnp.float32) * spread
    diag = jax.random.uniform(keys[1], (SUBS_SPAN, SUBS_CHORD, ROWS), jnp.float32, 1.2, 2.5)
    same = jnp.arange(ROWS)[:, None] == jnp.arange(ROWS)[None, :]
    return jnp.where(same, diag[..., :, None], off).astype(jnp.bfloat16)


def draw_displacement(key, part):
    keys = jax.random.split(jax.random.fold_in(key, 29), 1)
    shape = (SUBS_SPAN, SUBS_CHORD, ROWS, LOADS)
    ramp = (1.0 + 2.0 * jnp.arange(SUBS_SPAN, dtype=jnp.float32) / max(SUBS_SPAN - 1, 1)).reshape(SUBS_SPAN, 1, 1, 1)
    values = jax.random.normal(keys[0], shape, jnp.float32) * ramp
    return jnp.clip(values, -12.0, 12.0).astype(jnp.bfloat16)


def shard_levels(stream_key, extent, cuts, smallest, top_value):
    def one(position, shards_of):
        draws = jax.random.uniform(jax.random.fold_in(jax.random.fold_in(stream_key, 6), position), (shards_of,), jnp.float32, smallest / len(cuts), top_value / len(cuts))
        return jnp.repeat(jnp.exp(draws), extent[position] // shards_of).reshape((-1,) + (1,) * (len(extent) - position - 1))

    level = one(*cuts[0])
    for cut in cuts[1:]:
        level = level * one(*cut)
    return level


def setup_inputs(seed: int = 0) -> dict:
    key_list = jax.random.split(jax.random.key(seed), 9)
    return {
        "displacement": draw_displacement(jax.random.fold_in(key_list[8], 71), 0),
        "packed_blocks": draw_packed_blocks(jax.random.fold_in(key_list[8], 71), 0),
        "flex_scale": jnp.clip(jnp.exp(math.log(2.0) - 1.3862944 * jax.random.uniform(key_list[2], (SUBS_SPAN, SUBS_CHORD, ROWS), jnp.float32) ** shard_levels(key_list[2], (SUBS_SPAN, SUBS_CHORD, ROWS), ((0, 8), (1, 4)), -0.2, 0.2)), 0.5, 2.0),
        "dirichlet_scale": jnp.clip(jnp.exp(math.log(2.0) - 1.3862944 * jax.random.uniform(key_list[3], (SUBS_SPAN, SUBS_CHORD, ROWS), jnp.float32) ** shard_levels(key_list[3], (SUBS_SPAN, SUBS_CHORD, ROWS), ((0, 8), (1, 4)), -0.2, 0.2)), 0.5, 2.0),
        "dirichlet_diag": jnp.clip(1.1953125 + 1.3046875 * jax.random.uniform(key_list[4], (SUBS_SPAN, SUBS_CHORD, ROWS), jnp.float32) ** shard_levels(key_list[4], (SUBS_SPAN, SUBS_CHORD, ROWS), ((0, 8), (1, 4)), -0.2, 0.2), 1.1953125, 2.5).astype(jnp.bfloat16),
        "link_rows": draw_link_rows(jax.random.fold_in(key_list[8], 71), 0),
        "link_signs": draw_link_signs(jax.random.fold_in(key_list[8], 71), 0),
        "link_counts": draw_link_counts(jax.random.fold_in(key_list[8], 71), 0),
    }


def build_block(packed, diag, flex):
    size = packed.shape[0]
    row_ids = lax.broadcasted_iota(jnp.int32, (size, size), 0)
    col_ids = lax.broadcasted_iota(jnp.int32, (size, size), 1)
    mirror = packed.T
    if flex:
        return jnp.where(col_ids >= row_ids, packed, mirror)
    lower = jnp.where(row_ids > col_ids, packed, mirror)
    return jnp.where(row_ids == col_ids, diag[:, None], lower)

def local_term(block, scale, sign_row, field):
    operand = (scale[:, None] * sign_row[:, None] * field).astype(jnp.bfloat16)
    product = jnp.dot(block.astype(jnp.float32), operand.astype(jnp.float32), preferred_element_type=jnp.float32)
    return (sign_row[:, None] * scale[:, None] * product).astype(jnp.bfloat16)

def all_terms(packed_blocks, diag, scale, sign_rows, field, flex):
    lead = packed_blocks.shape[:2]
    count = lead[0] * lead[1]

    def single(items):
        block = build_block(items[0], items[1], flex)
        return local_term(block, items[2], items[3], items[4])
    terms = lax.map(single, (packed_blocks.reshape((count,) + packed_blocks.shape[2:]), diag.reshape(count, -1), scale.reshape(count, -1), sign_rows.reshape(count, -1), field.reshape((count,) + field.shape[2:])))
    return terms.reshape(lead + terms.shape[1:])

def live_slots(link_counts, slots):
    return lax.broadcasted_iota(jnp.int32, link_counts.shape + (slots,), 3) < link_counts[..., None]

def assemble(term, link_rows, link_counts):
    spans, chords, four, slots = link_rows.shape
    width = term.shape[-1]
    flat_rows = link_rows.reshape(spans, chords, four * slots).astype(jnp.int32)
    sent = jnp.take_along_axis(term, flat_rows[..., None], axis=2).reshape(spans, chords, four, slots, width)
    valid = live_slots(link_counts, slots)[..., None]
    sent = jnp.where(valid, sent, jnp.zeros_like(sent))
    zero_span = jnp.zeros_like(sent[:1, :, 0])
    zero_chord = jnp.zeros_like(sent[:, :1, 0])
    from_lower_span = jnp.concatenate([zero_span, sent[:-1, :, 1]], axis=0)
    from_upper_span = jnp.concatenate([sent[1:, :, 0], zero_span], axis=0)
    from_lower_chord = jnp.concatenate([zero_chord, sent[:, :-1, 3]], axis=1)
    from_upper_chord = jnp.concatenate([sent[:, 1:, 2], zero_chord], axis=1)
    received = jnp.stack([from_lower_span, from_upper_span, from_lower_chord, from_upper_chord], axis=2)
    received = jnp.where(valid, received, jnp.zeros_like(received))
    total = (sent.astype(jnp.float32) + received.astype(jnp.float32)).reshape(spans, chords, four * slots, width)

    def place(rows, values):
        return jnp.zeros((term.shape[2], width), jnp.float32).at[rows].set(values)
    return jax.vmap(jax.vmap(place))(flat_rows, total)

def make_sign_rows(link_rows, link_signs, link_counts, rows_total):
    spans, chords, four, slots = link_rows.shape
    valid = live_slots(link_counts, slots)
    values = jnp.where(valid, link_signs, 0).astype(jnp.float32).reshape(spans, chords, four * slots)
    flat_rows = link_rows.reshape(spans, chords, four * slots).astype(jnp.int32)

    def place(rows, vals):
        return jnp.zeros((rows_total,), jnp.float32).at[rows].set(vals)
    return jax.vmap(jax.vmap(place))(flat_rows, values)

def gram(left, right):
    return 0.5 * jnp.einsum('scrk,scrl->kl', left, right, precision=lax.Precision.HIGHEST)

def spd_solve(matrix, rhs):
    factor = jnp.linalg.cholesky(matrix)
    return jax.scipy.linalg.cho_solve((factor, True), rhs)

def mat_right(field, small):
    return jnp.einsum('scrk,kl->scrl', field, small, precision=lax.Precision.HIGHEST)

def reference(displacement, packed_blocks, flex_scale, dirichlet_scale, dirichlet_diag, link_rows, link_signs, link_counts):
    sign_rows = make_sign_rows(link_rows, link_signs, link_counts, packed_blocks.shape[2])

    def flex_apply(field):
        return assemble(all_terms(packed_blocks, dirichlet_diag, flex_scale, sign_rows, field, True), link_rows, link_counts)

    def dirichlet_apply(field):
        return assemble(all_terms(packed_blocks, dirichlet_diag, dirichlet_scale, sign_rows, field, False), link_rows, link_counts)
    gap_term = (sign_rows[..., None] * displacement.astype(jnp.float32)).astype(jnp.bfloat16)
    right = assemble(gap_term, link_rows, link_counts)
    multipliers = jnp.zeros_like(right)
    residual = right
    precond = dirichlet_apply(residual)
    direction = precond
    gamma = gram(precond, residual)
    for step in range(ITERS):
        image = flex_apply(direction)
        curv = gram(direction, image)
        alpha = spd_solve(curv, gamma)
        multipliers = multipliers + mat_right(direction, alpha)
        residual = residual - mat_right(image, alpha)
        if step + 1 < ITERS:
            precond = dirichlet_apply(residual)
            gamma_new = gram(precond, residual)
            beta = spd_solve(gamma, gamma_new)
            direction = precond + mat_right(direction, beta)
            gamma = gamma_new
    return (multipliers, residual)
```

```python
import functools

import jax
import jax.numpy as jnp
from jax import lax
from jax.experimental import pallas as pl
from jax.experimental.pallas import tpu as pltpu
from jax.sharding import PartitionSpec as P

MESH = pl.DeviceIdType.MESH
SIDES = (("span", -1), ("span", 1), ("chord", -1), ("chord", 1))
NT = (((1,), (1,)), ((), ()))


def digits(count):
    out, stride = [], 1
    while count > 1:
        if count % 4 == 0 and out:
            radix = 4
        else:
            radix = next(f for f in range(2, count + 1) if count % f == 0)
        out.append((radix, stride))
        stride *= radix
        count //= radix
    return out


def dot(a, b):
    return jnp.dot(a, b, preferred_element_type=jnp.float32)


def dot_nt(a, b):
    return lax.dot_general(a, b, NT, preferred_element_type=jnp.float32)


def fields_kernel(
    spans,
    chords,
    disp_ref,
    packed_ref,
    fscale_ref,
    dscale_ref,
    diag_ref,
    rows_ref,
    signs_ref,
    counts_ref,
    precond_ref,
    image_ref,
    residual_ref,
    gamma_ref,
    curv_ref,
    hot,
    fdiag,
    ddiag,
    sent,
    recv,
    acc,
    scattered,
    held,
    fan,
    full,
    side_send,
    side_recv,
    red_send,
    red_recv,
):
    size, loads = disp_ref.shape[2:]
    slots = rows_ref.shape[3]
    tile = fdiag.shape[1]
    tiles = size // tile
    pos = {"span": lax.axis_index("span"), "chord": lax.axis_index("chord")}
    limit = {"span": spans, "chord": chords}
    steps = digits(spans)
    chunk = loads // chords

    def chord_peer(k):
        return lax.rem(pos["chord"] + k, chords)

    def span_peer(radix, stride, k):
        digit = lax.rem(pos["span"] // stride, radix)
        return pos["span"] + (lax.rem(digit + k, radix) - digit) * stride

    barrier = pltpu.get_barrier_semaphore()
    greeted = [{"chord": chord_peer(k)} for k in range(1, chords)]
    greeted += [{"span": lax.rem(pos["span"] + k, spans)} for k in (1, spans - 1)]
    greeted += [
        {"span": span_peer(radix, stride, k)} for radix, stride in steps for k in range(1, radix)
    ]
    for device in greeted:
        pl.semaphore_signal(barrier, inc=1, device_id=device, device_id_type=MESH)

    live_signs = []
    for d in range(4):
        rows = rows_ref[0, 0, d : d + 1, :]
        row_ids = lax.broadcasted_iota(jnp.int32, (size, slots), 0)
        hot[:, d * slots : (d + 1) * slots] = jnp.where(row_ids == rows, 1.0, 0.0).astype(
            jnp.bfloat16
        )
        live = lax.broadcasted_iota(jnp.int32, (1, slots), 1) < counts_ref[0, 0, d]
        live_signs.append(
            jnp.where(live, signs_ref[0, 0, d : d + 1, :], 0).astype(jnp.float32)
        )
    signs = jnp.concatenate(live_signs, axis=1)
    signs = jnp.broadcast_to(signs, (16, size)).astype(jnp.bfloat16)
    sign = dot_nt(signs, hot[...])[0:1, :]

    def neighbour(d):
        axis, step = SIDES[d]
        other = pos[axis] + step
        return jnp.logical_and(other >= 0, other < limit[axis])

    def side_copy(e, d, slot):
        axis, step = SIDES[d]
        return pltpu.make_async_remote_copy(
            src_ref=sent.at[e, d],
            dst_ref=recv.at[e, slot],
            send_sem=side_send.at[e, d],
            recv_sem=side_recv.at[e, slot],
            device_id={axis: pos[axis] + step},
            device_id_type=MESH,
        )

    def send(e, term):
        values = dot(term, hot[...]).astype(jnp.bfloat16)
        for d in range(4):
            sent[e, d] = values[:, d * slots : (d + 1) * slots]
        for d in range(4):

            @pl.when(neighbour(d))
            def _():
                side_copy(e, d, d ^ 1).start()

    def partner(e):
        for d in range(4):

            @pl.when(neighbour(d))
            def _():
                side_copy(e, d, d).wait_recv()

        values = jnp.concatenate([recv[e, d] for d in range(4)], axis=1)
        return dot_nt(values, hot[...]).astype(jnp.bfloat16)

    def apply(diag_blocks, upper, scale, field):
        operand = (scale * sign * field).astype(jnp.bfloat16)
        out = []
        for b in range(tiles):
            lo, hi = b * tile, (b + 1) * tile
            total = dot(operand[:, lo:hi], diag_blocks[b])
            if upper:
                direct, mirrored = (0, lo), (hi, size)
            else:
                direct, mirrored = (hi, size), (0, lo)
            if direct[0] < direct[1]:
                total += dot(
                    operand[:, direct[0] : direct[1]],
                    packed_ref[0, 0, direct[0] : direct[1], lo:hi],
                )
            if mirrored[0] < mirrored[1]:
                total += dot_nt(
                    operand[:, mirrored[0] : mirrored[1]],
                    packed_ref[0, 0, lo:hi, mirrored[0] : mirrored[1]],
                )
            out.append(total)
        product = jnp.concatenate(out, axis=1)
        return (sign * scale * product).astype(jnp.bfloat16)

    def pair_gram(left, right):
        return sum(dot_nt(a, b) for a in left for b in right)

    def total_of(pair):
        return pair[0].astype(jnp.float32) + pair[1].astype(jnp.float32)

    class Reduction:
        def __init__(self, g):
            self.g, self.stage = g, 0

        def copy(self, n, src, dst, device):
            return pltpu.make_async_remote_copy(
                src_ref=src,
                dst_ref=dst,
                send_sem=red_send.at[self.g, n],
                recv_sem=red_recv.at[self.g, n],
                device_id=device,
                device_id_type=MESH,
            )

        def copies(self, stage):
            g, me = self.g, pos["chord"]
            if stage == 0:
                return [
                    self.copy(
                        k - 1,
                        acc.at[g, pl.ds(pl.multiple_of(chord_peer(k) * chunk, chunk), chunk)],
                        scattered.at[g, k - 1],
                        {"chord": chord_peer(k)},
                    )
                    for k in range(1, chords)
                ]
            first = chords - 1
            fans = [radix - 1 for radix, _ in steps]
            if stage <= len(steps):
                radix, stride = steps[stage - 1]
                base = sum(fans[: stage - 1])
                return [
                    self.copy(
                        first + base + k - 1,
                        held.at[g, stage - 1],
                        fan.at[g, base + k - 1],
                        {"span": span_peer(radix, stride, k)},
                    )
                    for k in range(1, radix)
                ]
            first += sum(fans)
            mine = pl.ds(pl.multiple_of(me * chunk, chunk), chunk)
            return [
                self.copy(
                    first + k - 1,
                    held.at[g, len(steps)],
                    full.at[g, mine],
                    {"chord": chord_peer(k)},
                )
                for k in range(1, chords)
            ]

        def start(self, value):
            acc[self.g] = value
            for copy in self.copies(0):
                copy.start()

        def advance(self):
            if self.stage > len(steps) + 1:
                return
            g, stage = self.g, self.stage
            copies = self.copies(stage)
            for copy in copies:
                copy.wait_recv()
            mine = pl.ds(pl.multiple_of(pos["chord"] * chunk, chunk), chunk)
            if stage == 0:
                total = acc[g, mine]
                for k in range(1, chords):
                    total += scattered[g, k - 1]
            elif stage <= len(steps):
                base = sum(radix - 1 for radix, _ in steps[: stage - 1])
                total = held[g, stage - 1]
                for k in range(steps[stage - 1][0] - 1):
                    total += fan[g, base + k]
            if stage <= len(steps):
                held[g, stage] = total
                if stage == len(steps):
                    full[g, mine] = total
                for copy in self.copies(stage + 1):
                    copy.start()
            self.stage += 1

        def finish(self):
            while self.stage <= len(steps) + 1:
                self.advance()
            for stage in range(len(steps) + 2):
                for copy in self.copies(stage):
                    copy.wait_send()

    disp = disp_ref[0, 0].astype(jnp.float32).T
    gap = (sign * disp).astype(jnp.bfloat16)
    for d in range(4):

        @pl.when(jnp.logical_not(neighbour(d)))
        def _():
            for e in range(3):
                recv[e, d] = jnp.zeros(recv.shape[2:], recv.dtype)

    pl.semaphore_wait(barrier, len(greeted))
    send(0, gap)
    for b in range(tiles):
        lo, hi = b * tile, (b + 1) * tile
        here = packed_ref[0, 0, lo:hi, lo:hi].astype(jnp.float32)
        mirror = here.T
        row_ids = lax.broadcasted_iota(jnp.int32, (tile, tile), 0)
        col_ids = lax.broadcasted_iota(jnp.int32, (tile, tile), 1)
        fdiag[b] = jnp.where(col_ids >= row_ids, here, mirror).astype(jnp.bfloat16)
        lower = jnp.where(row_ids > col_ids, here, mirror)
        diag = diag_ref[0, :, lo:hi].astype(jnp.float32)
        ddiag[b] = jnp.where(row_ids == col_ids, diag, lower).astype(jnp.bfloat16)
    fscale = fscale_ref[0]
    dscale = dscale_ref[0]

    right = (gap, partner(0))
    residual = total_of(right)
    term = apply(ddiag, False, dscale, residual)
    send(1, term)
    residual_ref[...] = residual.T
    precond = (term, partner(1))
    direction = total_of(precond)
    gamma = Reduction(0)
    gamma.start(pair_gram(precond, right))
    term = apply(fdiag, True, fscale, direction)
    send(2, term)
    gamma.advance()
    precond_ref[...] = direction.T
    image = (term, partner(2))
    curv = Reduction(1)
    curv.start(pair_gram(precond, image))
    gamma.advance()
    image_ref[...] = total_of(image).T
    curv.advance()
    gamma.advance()
    curv.advance()
    gamma.advance()
    curv.finish()
    gamma.finish()
    gamma_ref[...] = full[0]
    curv_ref[...] = full[1]
    for e in range(3):
        for d in range(4):

            @pl.when(neighbour(d))
            def _():
                side_copy(e, d, d).wait_send()


def update_kernel(precond_ref, image_ref, residual_ref, gamma_ref, curv_ref, mult_ref, res_ref):
    loads = curv_ref.shape[0]
    width = 8
    matrix = curv_ref[...]
    matrix = 0.5 * (matrix + matrix.T)
    rhs = gamma_ref[...]
    count = loads // width
    left = [matrix[p * width : (p + 1) * width] for p in range(count)]
    right = [rhs[p * width : (p + 1) * width] for p in range(count)]
    shape = (width, loads)
    sub_ids = lax.broadcasted_iota(jnp.int32, shape, 0)

    def column(block, c):
        return jnp.broadcast_to(block[:, c : c + 1], shape)

    def row(block, r):
        return jnp.broadcast_to(block[r : r + 1, :], shape)

    for p in range(count):
        here, there = left[p], right[p]
        cols = [column(here, p * width + j) for j in range(width)]
        for j in range(width):
            inverse = 1.0 / row(cols[j], j)

            def eliminate(block):
                pivot = row(block, j) * inverse
                return jnp.where(sub_ids == j, pivot, block - cols[j] * pivot)

            here, there = eliminate(here), eliminate(there)
            cols = cols[: j + 1] + [eliminate(c) for c in cols[j + 1 :]]
        left[p], right[p] = here, there
        rows_left = [row(here, j) for j in range(width)]
        rows_right = [row(there, j) for j in range(width)]
        order = [(p + k) % count for k in range(1, count)]
        for r in order:
            factors = [column(left[r], p * width + j) for j in range(width)]
            for j in range(width):
                right[r] = right[r] - factors[j] * rows_right[j]
            if p + 1 < count:
                for j in range(width):
                    left[r] = left[r] - factors[j] * rows_left[j]
    alpha = jnp.concatenate(right, axis=0)

    def mat_right(field):
        return jnp.dot(
            field, alpha, precision=lax.Precision.HIGHEST, preferred_element_type=jnp.float32
        )

    mult_ref[0, 0] = mat_right(precond_ref[...])
    res_ref[0, 0] = residual_ref[...] - mat_right(image_ref[...])


def shards(spans, chords, *args):
    displacement, packed, link_rows = args[0], args[1], args[5]
    size, loads = displacement.shape[2:]
    slots = link_rows.shape[3]
    tile = min(256, size)
    steps = digits(spans)
    fans = sum(radix - 1 for radix, _ in steps)
    sems = 2 * (chords - 1) + fans
    chunk = loads // chords
    f32, bf16 = jnp.float32, jnp.bfloat16
    vmem = pl.BlockSpec(memory_space=pltpu.VMEM)
    smem = pl.BlockSpec(memory_space=pltpu.SMEM)
    field = jax.ShapeDtypeStruct((size, loads), f32)
    small = jax.ShapeDtypeStruct((loads, loads), f32)
    middle = pl.pallas_call(
        functools.partial(fields_kernel, spans, chords),
        out_shape=(field, field, field, small, small),
        in_specs=[vmem] * 7 + [smem],
        out_specs=(vmem,) * 5,
        scratch_shapes=[
            pltpu.VMEM((size, size), bf16),
            pltpu.VMEM((size // tile, tile, tile), bf16),
            pltpu.VMEM((size // tile, tile, tile), bf16),
            pltpu.VMEM((3, 4, loads, slots), bf16),
            pltpu.VMEM((3, 4, loads, slots), bf16),
            pltpu.VMEM((2, loads, loads), f32),
            pltpu.VMEM((2, chords - 1, chunk, loads), f32),
            pltpu.VMEM((2, len(steps) + 1, chunk, loads), f32),
            pltpu.VMEM((2, fans, chunk, loads), f32),
            pltpu.VMEM((2, loads, loads), f32),
            pltpu.SemaphoreType.DMA((3, 4)),
            pltpu.SemaphoreType.DMA((3, 4)),
            pltpu.SemaphoreType.DMA((2, sems)),
            pltpu.SemaphoreType.DMA((2, sems)),
        ],
        compiler_params=pltpu.CompilerParams(
            collective_id=0, has_side_effects=True, vmem_limit_bytes=40 * 1024 * 1024
        ),
        name="fields",
    )(*args)
    out = jax.ShapeDtypeStruct((1, 1, size, loads), f32)
    return pl.pallas_call(
        update_kernel,
        out_shape=(out, out),
        in_specs=[vmem] * 5,
        out_specs=(vmem, vmem),
        compiler_params=pltpu.CompilerParams(vmem_limit_bytes=40 * 1024 * 1024),
        name="update",
    )(*middle)


def solution(mesh):
    wide = P("span", "chord", None, None)
    narrow = P("span", "chord", None)
    return jax.shard_map(
        functools.partial(shards, mesh.shape["span"], mesh.shape["chord"]),
        mesh=mesh,
        in_specs=(wide, wide, narrow, narrow, narrow, wide, wide, narrow),
        out_specs=(wide, wide),
        check_vma=False,
    )
```

```python
import functools

import jax
import jax.numpy as jnp
from jax import lax
from jax.experimental import pallas as pl
from jax.experimental.pallas import tpu as pltpu
from jax.sharding import PartitionSpec as P

MESH = pl.DeviceIdType.MESH
SIDES = (("span", -1), ("span", 1), ("chord", -1), ("chord", 1))
NT = (((1,), (1,)), ((), ()))


def digits(count):
    out, stride = [], 1
    while count > 1:
        if count % 4 == 0 and out:
            radix = 4
        else:
            radix = next(f for f in range(2, count + 1) if count % f == 0)
        out.append((radix, stride))
        stride *= radix
        count //= radix
    return out


def dot(a, b):
    return jnp.dot(a, b, preferred_element_type=jnp.float32)


def dot_nt(a, b):
    return lax.dot_general(a, b, NT, preferred_element_type=jnp.float32)


def fields_kernel(
    spans,
    chords,
    *refs,
):
    inputs, refs = refs[:8], refs[8:]
    outputs = refs[:5]
    local, refs = refs[5:13], refs[13:]
    disp_ref, packed_ref, fscale_ref, dscale_ref, diag_ref, rows_ref, signs_ref, counts_ref = local
    (
    hot,
    fdiag,
    ddiag,
    sent,
    recv,
    acc,
    scattered,
    held,
    fan,
    full,
    side_send,
    side_recv,
    red_send,
    red_recv,
    load_sem,
    precond_ref,
    image_ref,
    residual_ref,
    store_sem,
    ) = refs
    size, loads = disp_ref.shape[2:]
    slots = rows_ref.shape[3]
    tile = fdiag.shape[1]
    tiles = size // tile
    pos = {"span": lax.axis_index("span"), "chord": lax.axis_index("chord")}
    limit = {"span": spans, "chord": chords}
    (near, _), *steps = digits(spans)
    group = chords * near
    chunk = loads // group

    loading = [
        pltpu.make_async_copy(inputs[n], local[n], load_sem.at[n]) for n in range(8)
    ]
    for n in (5, 0, 6, 7, 1, 3, 4, 2):
        loading[n].start()

    def span_peer(radix, stride, k):
        digit = lax.rem(pos["span"] // stride, radix)
        return pos["span"] + (lax.rem(digit + k, radix) - digit) * stride

    def group_peer(m):
        chord = lax.rem(pos["chord"] + m // near, chords)
        device = {"span": span_peer(near, 1, m % near), "chord": chord}
        return device, chord * near + lax.rem(device["span"], near)

    mine = pl.ds(
        pl.multiple_of((pos["chord"] * near + lax.rem(pos["span"], near)) * chunk, chunk), chunk
    )

    barrier = pltpu.get_barrier_semaphore()
    greeted = [group_peer(m)[0] for m in range(1, group)]
    greeted += [{"span": lax.rem(pos["span"] + k, spans)} for k in (1, spans - 1)]
    greeted += [
        {"span": span_peer(radix, stride, k)} for radix, stride in steps for k in range(1, radix)
    ]
    for device in greeted:
        pl.semaphore_signal(barrier, inc=1, device_id=device, device_id_type=MESH)

    for n in (5, 6, 7):
        loading[n].wait()
    live_signs = []
    for d in range(4):
        rows = rows_ref[0, 0, d : d + 1, :]
        row_ids = lax.broadcasted_iota(jnp.int32, (size, slots), 0)
        hot[:, d * slots : (d + 1) * slots] = jnp.where(row_ids == rows, 1.0, 0.0).astype(
            jnp.bfloat16
        )
        live = lax.broadcasted_iota(jnp.int32, (1, slots), 1) < counts_ref[0, :, d : d + 1]
        live_signs.append(
            jnp.where(live, signs_ref[0, 0, d : d + 1, :], 0).astype(jnp.float32)
        )
    slot_sign = jnp.concatenate(live_signs, axis=1)

    def neighbour(d):
        axis, step = SIDES[d]
        other = pos[axis] + step
        return jnp.logical_and(other >= 0, other < limit[axis])

    def side_copy(e, d, slot):
        axis, step = SIDES[d]
        return pltpu.make_async_remote_copy(
            src_ref=sent.at[e, d],
            dst_ref=recv.at[e, slot],
            send_sem=side_send.at[e, d],
            recv_sem=side_recv.at[e, slot],
            device_id={axis: pos[axis] + step},
            device_id_type=MESH,
        )

    def send(e, term, scale=None):
        for pair in ((0, 1), (2, 3)):
            here = slice(pair[0] * slots, (pair[1] + 1) * slots)
            values = dot(term, hot[:, here])
            if scale is not None:
                values = values * scale[:, here]
            values = values.astype(jnp.bfloat16)
            for d in pair:
                sent[e, d] = values[:, (d - pair[0]) * slots : (d - pair[0] + 1) * slots]

                @pl.when(neighbour(d))
                def _():
                    side_copy(e, d, d ^ 1).start()

    def partner(e):
        total = 0
        for pair in ((2, 3), (0, 1)):
            for d in pair:

                @pl.when(neighbour(d))
                def _():
                    side_copy(e, d, d).wait_recv()

            values = jnp.concatenate([recv[e, d] for d in pair], axis=1)
            total += dot_nt(values, hot[:, pair[0] * slots : (pair[1] + 1) * slots])
        return total.astype(jnp.bfloat16)

    def apply(diag_blocks, upper, scale, field):
        operand = (scale * sign * field).astype(jnp.bfloat16)
        out = []
        for b in range(tiles):
            lo, hi = b * tile, (b + 1) * tile
            total = dot(operand[:, lo:hi], diag_blocks[b])
            if upper:
                direct, mirrored = (0, lo), (hi, size)
            else:
                direct, mirrored = (hi, size), (0, lo)
            if direct[0] < direct[1]:
                total += dot(
                    operand[:, direct[0] : direct[1]],
                    packed_ref[0, 0, direct[0] : direct[1], lo:hi],
                )
            if mirrored[0] < mirrored[1]:
                total += dot_nt(
                    operand[:, mirrored[0] : mirrored[1]],
                    packed_ref[0, 0, lo:hi, mirrored[0] : mirrored[1]],
                )
            out.append(total)
        product = jnp.concatenate(out, axis=1)
        return (sign * scale * product).astype(jnp.bfloat16)

    def pair_gram(left, right):
        return sum(dot_nt(a, b) for a in left for b in right)

    def total_of(pair):
        return pair[0].astype(jnp.float32) + pair[1].astype(jnp.float32)

    class Reduction:
        def __init__(self, g):
            self.g, self.stage = g, 0

        def copy(self, n, src, dst, device):
            return pltpu.make_async_remote_copy(
                src_ref=src,
                dst_ref=dst,
                send_sem=red_send.at[self.g, n],
                recv_sem=red_recv.at[self.g, n],
                device_id=device,
                device_id_type=MESH,
            )

        def copies(self, stage):
            g = self.g
            if stage == 0:
                out = []
                for m in range(1, group):
                    device, owner = group_peer(m)
                    rows = pl.ds(pl.multiple_of(owner * chunk, chunk), chunk)
                    out.append(self.copy(m - 1, acc.at[g, rows], scattered.at[g, m - 1], device))
                return out
            first = group - 1
            fans = [radix - 1 for radix, _ in steps]
            if stage <= len(steps):
                radix, stride = steps[stage - 1]
                base = sum(fans[: stage - 1])
                return [
                    self.copy(
                        first + base + k - 1,
                        held.at[g, stage - 1],
                        fan.at[g, base + k - 1],
                        {"span": span_peer(radix, stride, k)},
                    )
                    for k in range(1, radix)
                ]
            first += sum(fans)
            return [
                self.copy(
                    first + m - 1, held.at[g, len(steps)], full.at[g, mine], group_peer(m)[0]
                )
                for m in range(1, group)
            ]

        def start(self, value):
            acc[self.g] = value
            for copy in self.copies(0):
                copy.start()

        def advance(self):
            if self.stage > len(steps) + 1:
                return
            g, stage = self.g, self.stage
            copies = self.copies(stage)
            for copy in copies:
                copy.wait_recv()
            if stage == 0:
                total = acc[g, mine]
                for m in range(1, group):
                    total += scattered[g, m - 1]
            elif stage <= len(steps):
                base = sum(radix - 1 for radix, _ in steps[: stage - 1])
                total = held[g, stage - 1]
                for k in range(steps[stage - 1][0] - 1):
                    total += fan[g, base + k]
            if stage <= len(steps):
                held[g, stage] = total
                if stage == len(steps):
                    full[g, mine] = total
                for copy in self.copies(stage + 1):
                    copy.start()
            self.stage += 1

        def finish(self):
            while self.stage <= len(steps) + 1:
                self.advance()
            for stage in range(len(steps) + 2):
                for copy in self.copies(stage):
                    copy.wait_send()

    def lay(ref, pair):
        for n, part in enumerate(pair):
            ref[:, n * loads : (n + 1) * loads] = part.astype(jnp.float32).T.astype(ref.dtype)

    stored = (precond_ref, image_ref, residual_ref, full.at[0], full.at[1])
    storing = [
        pltpu.make_async_copy(stored[n], outputs[n], store_sem.at[n]) for n in range(5)
    ]

    loading[0].wait()
    disp = disp_ref[0, 0].astype(jnp.float32).T
    for d in range(4):

        @pl.when(jnp.logical_not(neighbour(d)))
        def _():
            for e in range(3):
                recv[e, d] = jnp.zeros(recv.shape[2:], recv.dtype)

    pl.semaphore_wait(barrier, len(greeted))
    send(0, disp.astype(jnp.bfloat16), slot_sign)
    signs = jnp.broadcast_to(slot_sign, (16, size)).astype(jnp.bfloat16)
    sign = dot_nt(signs, hot[...])[0:1, :]
    gap = (sign * disp).astype(jnp.bfloat16)
    for n in (1, 2, 3, 4):
        loading[n].wait()
    for b in range(tiles):
        lo, hi = b * tile, (b + 1) * tile
        here = packed_ref[0, 0, lo:hi, lo:hi].astype(jnp.float32)
        mirror = here.T
        row_ids = lax.broadcasted_iota(jnp.int32, (tile, tile), 0)
        col_ids = lax.broadcasted_iota(jnp.int32, (tile, tile), 1)
        fdiag[b] = jnp.where(col_ids >= row_ids, here, mirror).astype(jnp.bfloat16)
        lower = jnp.where(row_ids > col_ids, here, mirror)
        diag = diag_ref[0, :, lo:hi].astype(jnp.float32)
        ddiag[b] = jnp.where(row_ids == col_ids, diag, lower).astype(jnp.bfloat16)
    fscale = fscale_ref[0]
    dscale = dscale_ref[0]

    right = (gap, partner(0))
    residual = total_of(right)
    term = apply(ddiag, False, dscale, residual)
    send(1, term)
    residual_ref[...] = residual.T
    storing[2].start()
    precond = (term, partner(1))
    direction = total_of(precond)
    gamma = Reduction(0)
    gamma.start(pair_gram(precond, right))
    term = apply(fdiag, True, fscale, direction)
    send(2, term)
    gamma.advance()
    lay(precond_ref, precond)
    storing[0].start()
    early = pair_gram(precond, (term,))
    image = (term, partner(2))
    curv = Reduction(1)
    curv.start(early + pair_gram(precond, image[1:]))
    gamma.advance()
    lay(image_ref, image)
    storing[1].start()
    curv.advance()
    gamma.advance()
    curv.advance()
    gamma.advance()
    gamma.finish()
    storing[3].start()
    curv.finish()
    storing[4].start()
    for e in range(3):
        for d in range(4):

            @pl.when(neighbour(d))
            def _():
                side_copy(e, d, d).wait_send()

    for copy in storing:
        copy.wait()


def update_kernel(*refs):
    inputs, outputs, local = refs[:5], refs[5:7], refs[7:14]
    load_sem, store_sem = refs[14:]
    precond_ref, image_ref, residual_ref, gamma_ref, curv_ref, mult_ref, res_ref = local
    loading = [
        pltpu.make_async_copy(inputs[n], local[n], load_sem.at[n]) for n in range(5)
    ]
    storing = [
        pltpu.make_async_copy(local[5 + n], outputs[n].at[0, 0], store_sem.at[n]) for n in range(2)
    ]
    for copy in loading[::-1]:
        copy.start()
    for copy in loading[3:]:
        copy.wait()
    loads = curv_ref.shape[0]
    width = 8
    matrix = curv_ref[...]
    matrix = 0.5 * (matrix + matrix.T)
    rhs = gamma_ref[...]
    count = loads // width
    left = [matrix[p * width : (p + 1) * width] for p in range(count)]
    right = [rhs[p * width : (p + 1) * width] for p in range(count)]
    shape = (width, loads)
    sub_ids = lax.broadcasted_iota(jnp.int32, shape, 0)

    def column(block, c):
        return jnp.broadcast_to(block[:, c : c + 1], shape)

    def row(block, r):
        return jnp.broadcast_to(block[r : r + 1, :], shape)

    for p in range(count):
        here, there = left[p], right[p]
        cols = [column(here, p * width + j) for j in range(width)]
        for j in range(width):
            inverse = 1.0 / row(cols[j], j)

            def eliminate(block):
                pivot = row(block, j) * inverse
                return jnp.where(sub_ids == j, pivot, block - cols[j] * pivot)

            here, there = eliminate(here), eliminate(there)
            cols = cols[: j + 1] + [eliminate(c) for c in cols[j + 1 :]]
        left[p], right[p] = here, there
        rows_left = [row(here, j) for j in range(width)]
        rows_right = [row(there, j) for j in range(width)]
        order = [(p + k) % count for k in range(1, count)]
        for r in order:
            factors = [column(left[r], p * width + j) for j in range(width)]
            for j in range(width):
                right[r] = right[r] - factors[j] * rows_right[j]
            if p + 1 < count:
                for j in range(width):
                    left[r] = left[r] - factors[j] * rows_left[j]
    alpha = jnp.concatenate(right, axis=0)

    high = alpha.astype(jnp.bfloat16)
    low = (alpha - high.astype(jnp.float32)).astype(jnp.bfloat16)
    parts = jnp.concatenate([high, low], axis=1)
    parts = jnp.concatenate([parts, parts], axis=0)

    def mat_right(pair):
        both = dot(pair, parts)
        return both[:, :loads] + both[:, loads:]

    for copy in loading[:3]:
        copy.wait()
    mult_ref[...] = mat_right(precond_ref[...])
    storing[0].start()
    res_ref[...] = residual_ref[...] - mat_right(image_ref[...])
    storing[1].start()
    for copy in storing:
        copy.wait()


def shards(spans, chords, *args):
    displacement, packed, link_rows = args[0], args[1], args[5]
    size, loads = displacement.shape[2:]
    slots = link_rows.shape[3]
    tile = min(256, size)
    (near, _), *steps = digits(spans)
    fans = sum(radix - 1 for radix, _ in steps)
    group = chords * near
    sems = 2 * (group - 1) + fans
    chunk = loads // group
    f32, bf16 = jnp.float32, jnp.bfloat16
    hbm = pl.BlockSpec(memory_space=pltpu.HBM)
    pair = jax.ShapeDtypeStruct((size, 2 * loads), bf16)
    field = jax.ShapeDtypeStruct((size, loads), f32)
    small = jax.ShapeDtypeStruct((loads, loads), f32)
    middle = pl.pallas_call(
        functools.partial(fields_kernel, spans, chords),
        out_shape=(pair, pair, field, small, small),
        in_specs=[hbm] * 8,
        out_specs=(hbm,) * 5,
        scratch_shapes=[pltpu.VMEM(a.shape, a.dtype) for a in args]
        + [
            pltpu.VMEM((size, size), bf16),
            pltpu.VMEM((size // tile, tile, tile), bf16),
            pltpu.VMEM((size // tile, tile, tile), bf16),
            pltpu.VMEM((3, 4, loads, slots), bf16),
            pltpu.VMEM((3, 4, loads, slots), bf16),
            pltpu.VMEM((2, loads, loads), f32),
            pltpu.VMEM((2, group - 1, chunk, loads), f32),
            pltpu.VMEM((2, len(steps) + 1, chunk, loads), f32),
            pltpu.VMEM((2, max(fans, 1), chunk, loads), f32),
            pltpu.VMEM((2, loads, loads), f32),
            pltpu.SemaphoreType.DMA((3, 4)),
            pltpu.SemaphoreType.DMA((3, 4)),
            pltpu.SemaphoreType.DMA((2, sems)),
            pltpu.SemaphoreType.DMA((2, sems)),
            pltpu.SemaphoreType.DMA((8,)),
            pltpu.VMEM(pair.shape, pair.dtype),
            pltpu.VMEM(pair.shape, pair.dtype),
            pltpu.VMEM(field.shape, field.dtype),
            pltpu.SemaphoreType.DMA((5,)),
        ],
        compiler_params=pltpu.CompilerParams(
            collective_id=0, has_side_effects=True, vmem_limit_bytes=60 * 1024 * 1024
        ),
        name="fields",
    )(*args)
    out = jax.ShapeDtypeStruct((1, 1, size, loads), f32)
    return pl.pallas_call(
        update_kernel,
        out_shape=(out, out),
        in_specs=[hbm] * 5,
        out_specs=(hbm, hbm),
        scratch_shapes=[
            pltpu.VMEM(a.shape, a.dtype) for a in (pair, pair, field, small, small, field, field)
        ]
        + [pltpu.SemaphoreType.DMA((5,)), pltpu.SemaphoreType.DMA((2,))],
        compiler_params=pltpu.CompilerParams(vmem_limit_bytes=60 * 1024 * 1024),
        name="update",
    )(*middle)


def solution(mesh):
    wide = P("span", "chord", None, None)
    narrow = P("span", "chord", None)
    return jax.shard_map(
        functools.partial(shards, mesh.shape["span"], mesh.shape["chord"]),
        mesh=mesh,
        in_specs=(wide, wide, narrow, narrow, narrow, wide, wide, narrow),
        out_specs=(wide, wide),
        check_vma=False,
    )
```

```python
import functools

import jax
import jax.numpy as jnp
from jax import lax
from jax.experimental import pallas as pl
from jax.experimental.pallas import tpu as pltpu
from jax.sharding import PartitionSpec as P

MESH = pl.DeviceIdType.MESH
SIDES = (("span", -1), ("span", 1), ("chord", -1), ("chord", 1))
NT = (((1,), (1,)), ((), ()))


def digits(count):
    out, stride = [], 1
    while count > 1:
        if count % 4 == 0 and out:
            radix = 4
        else:
            radix = next(f for f in range(2, count + 1) if count % f == 0)
        out.append((radix, stride))
        stride *= radix
        count //= radix
    return out


def dot(a, b):
    return jnp.dot(a, b, preferred_element_type=jnp.float32)


def dot_nt(a, b):
    return lax.dot_general(a, b, NT, preferred_element_type=jnp.float32)


def fields_kernel(
    spans,
    chords,
    *refs,
):
    inputs, refs = refs[:8], refs[8:]
    outputs = refs[:5]
    local, refs = refs[5:13], refs[13:]
    disp_ref, packed_ref, fscale_ref, dscale_ref, diag_ref, rows_ref, signs_ref, counts_ref = local
    (
    hot,
    fdiag,
    ddiag,
    sent,
    recv,
    acc,
    scattered,
    held,
    fan,
    full,
    side_send,
    side_recv,
    red_send,
    red_recv,
    load_sem,
    precond_ref,
    image_ref,
    residual_ref,
    store_sem,
    ) = refs
    size, loads = disp_ref.shape[2:]
    slots = rows_ref.shape[3]
    half = sent.shape[3]
    parts = loads // half
    tile = fdiag.shape[1]
    tiles = size // tile
    pos = {"span": lax.axis_index("span"), "chord": lax.axis_index("chord")}
    limit = {"span": spans, "chord": chords}
    (near, _), *steps = digits(spans)
    group = chords * near
    chunk = loads // group

    loading = [
        pltpu.make_async_copy(inputs[n], local[n], load_sem.at[n]) for n in range(8)
    ]
    for n in (5, 0, 6, 7, 1, 3, 4, 2):
        loading[n].start()

    def span_peer(radix, stride, k):
        digit = lax.rem(pos["span"] // stride, radix)
        return pos["span"] + (lax.rem(digit + k, radix) - digit) * stride

    def group_peer(m):
        chord = lax.rem(pos["chord"] + m // near, chords)
        device = {"span": span_peer(near, 1, m % near), "chord": chord}
        return device, chord * near + lax.rem(device["span"], near)

    mine = pl.ds(
        pl.multiple_of((pos["chord"] * near + lax.rem(pos["span"], near)) * chunk, chunk), chunk
    )

    barrier = pltpu.get_barrier_semaphore()
    greeted = [group_peer(m)[0] for m in range(1, group)]
    greeted += [{"span": lax.rem(pos["span"] + k, spans)} for k in (1, spans - 1)]
    greeted += [
        {"span": span_peer(radix, stride, k)} for radix, stride in steps for k in range(1, radix)
    ]
    for device in greeted:
        pl.semaphore_signal(barrier, inc=1, device_id=device, device_id_type=MESH)

    for n in (5, 6, 7):
        loading[n].wait()
    live_signs = []
    for d in range(4):
        rows = rows_ref[0, 0, d : d + 1, :]
        row_ids = lax.broadcasted_iota(jnp.int32, (size, slots), 0)
        hot[:, d * slots : (d + 1) * slots] = jnp.where(row_ids == rows, 1.0, 0.0).astype(
            jnp.bfloat16
        )
        live = lax.broadcasted_iota(jnp.int32, (1, slots), 1) < counts_ref[0, :, d : d + 1]
        live_signs.append(
            jnp.where(live, signs_ref[0, 0, d : d + 1, :], 0).astype(jnp.float32)
        )
    slot_sign = jnp.concatenate(live_signs, axis=1)

    def neighbour(d):
        axis, step = SIDES[d]
        other = pos[axis] + step
        return jnp.logical_and(other >= 0, other < limit[axis])

    def side_copy(e, h, d, slot):
        axis, step = SIDES[d]
        return pltpu.make_async_remote_copy(
            src_ref=sent.at[e, h, d],
            dst_ref=recv.at[e, h, slot],
            send_sem=side_send.at[e, h, d],
            recv_sem=side_recv.at[e, h, slot],
            device_id={axis: pos[axis] + step},
            device_id_type=MESH,
        )

    def send(e, halves, term, scale=None):
        for pair in ((0, 1), (2, 3)):
            here = slice(pair[0] * slots, (pair[1] + 1) * slots)
            values = dot(term, hot[:, here])
            if scale is not None:
                values = values * scale[:, here]
            values = values.astype(jnp.bfloat16)
            for n, h in enumerate(halves):
                for d in pair:
                    sent[e, h, d] = values[
                        n * half : (n + 1) * half,
                        (d - pair[0]) * slots : (d - pair[0] + 1) * slots,
                    ]

                    @pl.when(neighbour(d))
                    def _():
                        side_copy(e, h, d, d ^ 1).start()

    def partner(e, halves):
        total = 0
        for pair in ((2, 3), (0, 1)):
            for d in pair:

                @pl.when(neighbour(d))
                def _():
                    for h in halves:
                        side_copy(e, h, d, d).wait_recv()

            values = [jnp.concatenate([recv[e, h, d] for d in pair], axis=1) for h in halves]
            total += dot_nt(
                jnp.concatenate(values, axis=0), hot[:, pair[0] * slots : (pair[1] + 1) * slots]
            )
        return total.astype(jnp.bfloat16)

    def apply(diag_blocks, upper, scale, field):
        operand = (scale * sign * field).astype(jnp.bfloat16)
        out = []
        for b in range(tiles):
            lo, hi = b * tile, (b + 1) * tile
            total = dot(operand[:, lo:hi], diag_blocks[b])
            if upper:
                direct, mirrored = (0, lo), (hi, size)
            else:
                direct, mirrored = (hi, size), (0, lo)
            if direct[0] < direct[1]:
                total += dot(
                    operand[:, direct[0] : direct[1]],
                    packed_ref[0, 0, direct[0] : direct[1], lo:hi],
                )
            if mirrored[0] < mirrored[1]:
                total += dot_nt(
                    operand[:, mirrored[0] : mirrored[1]],
                    packed_ref[0, 0, lo:hi, mirrored[0] : mirrored[1]],
                )
            out.append(total)
        product = jnp.concatenate(out, axis=1)
        return (sign * scale * product).astype(jnp.bfloat16)

    def pair_gram(left, right):
        return sum(dot_nt(a, b) for a in left for b in right)

    def total_of(pair):
        return pair[0].astype(jnp.float32) + pair[1].astype(jnp.float32)

    class Reduction:
        def __init__(self, g):
            self.g, self.stage = g, 0

        def copy(self, n, src, dst, device):
            return pltpu.make_async_remote_copy(
                src_ref=src,
                dst_ref=dst,
                send_sem=red_send.at[self.g, n],
                recv_sem=red_recv.at[self.g, n],
                device_id=device,
                device_id_type=MESH,
            )

        def copies(self, stage):
            g = self.g
            if stage == 0:
                out = []
                for m in range(1, group):
                    device, owner = group_peer(m)
                    rows = pl.ds(pl.multiple_of(owner * chunk, chunk), chunk)
                    out.append(self.copy(m - 1, acc.at[g, rows], scattered.at[g, m - 1], device))
                return out
            first = group - 1
            fans = [radix - 1 for radix, _ in steps]
            if stage <= len(steps):
                radix, stride = steps[stage - 1]
                base = sum(fans[: stage - 1])
                return [
                    self.copy(
                        first + base + k - 1,
                        held.at[g, stage - 1],
                        fan.at[g, base + k - 1],
                        {"span": span_peer(radix, stride, k)},
                    )
                    for k in range(1, radix)
                ]
            first += sum(fans)
            return [
                self.copy(
                    first + m - 1, held.at[g, len(steps)], full.at[g, mine], group_peer(m)[0]
                )
                for m in range(1, group)
            ]

        def start(self, value):
            acc[self.g] = value
            for copy in self.copies(0):
                copy.start()

        def advance(self):
            if self.stage > len(steps) + 1:
                return
            g, stage = self.g, self.stage
            copies = self.copies(stage)
            for copy in copies:
                copy.wait_recv()
            if stage == 0:
                total = acc[g, mine]
                for m in range(1, group):
                    total += scattered[g, m - 1]
            elif stage <= len(steps):
                base = sum(radix - 1 for radix, _ in steps[: stage - 1])
                total = held[g, stage - 1]
                for k in range(steps[stage - 1][0] - 1):
                    total += fan[g, base + k]
            if stage <= len(steps):
                held[g, stage] = total
                if stage == len(steps):
                    full[g, mine] = total
                for copy in self.copies(stage + 1):
                    copy.start()
            self.stage += 1

        def finish(self):
            while self.stage <= len(steps) + 1:
                self.advance()
            for stage in range(len(steps) + 2):
                for copy in self.copies(stage):
                    copy.wait_send()

    def lay(ref, pair):
        for n, part in enumerate(pair):
            ref[:, n * loads : (n + 1) * loads] = part.astype(jnp.float32).T.astype(ref.dtype)

    stored = (precond_ref, image_ref, residual_ref, full.at[0], full.at[1])
    storing = [
        pltpu.make_async_copy(stored[n], outputs[n], store_sem.at[n]) for n in range(5)
    ]

    loading[0].wait()
    disp = disp_ref[0, 0].astype(jnp.float32).T
    for d in range(4):

        @pl.when(jnp.logical_not(neighbour(d)))
        def _():
            for e in range(3):
                for h in range(parts):
                    recv[e, h, d] = jnp.zeros(recv.shape[3:], recv.dtype)

    pl.semaphore_wait(barrier, len(greeted))
    send(0, range(parts), disp.astype(jnp.bfloat16), slot_sign)
    signs = jnp.broadcast_to(slot_sign, (16, size)).astype(jnp.bfloat16)
    sign = dot_nt(signs, hot[...])[0:1, :]
    gap = (sign * disp).astype(jnp.bfloat16)
    for n in (1, 2, 3, 4):
        loading[n].wait()
    for b in range(tiles):
        lo, hi = b * tile, (b + 1) * tile
        here = packed_ref[0, 0, lo:hi, lo:hi].astype(jnp.float32)
        mirror = here.T
        row_ids = lax.broadcasted_iota(jnp.int32, (tile, tile), 0)
        col_ids = lax.broadcasted_iota(jnp.int32, (tile, tile), 1)
        fdiag[b] = jnp.where(col_ids >= row_ids, here, mirror).astype(jnp.bfloat16)
        lower = jnp.where(row_ids > col_ids, here, mirror)
        diag = diag_ref[0, :, lo:hi].astype(jnp.float32)
        ddiag[b] = jnp.where(row_ids == col_ids, diag, lower).astype(jnp.bfloat16)
    fscale = fscale_ref[0]
    dscale = dscale_ref[0]

    def rows_of(pieces):
        return tuple(jnp.concatenate([p[n] for p in pieces], axis=0) for n in range(2))

    right, terms = [], []
    for h in range(parts):
        right.append((gap[h * half : (h + 1) * half], partner(0, (h,))))
        terms.append(apply(ddiag, False, dscale, total_of(right[h])))
        send(1, (h,), terms[h])
    right = rows_of(right)
    residual_ref[...] = total_of(right).T
    storing[2].start()
    precond, images = [], []
    for h in range(parts):
        precond.append((terms[h], partner(1, (h,))))
        images.append(apply(fdiag, True, fscale, total_of(precond[h])))
        send(2, (h,), images[h])
    precond = rows_of(precond)
    gamma = Reduction(0)
    gamma.start(pair_gram(precond, right))
    lay(precond_ref, precond)
    storing[0].start()
    term = jnp.concatenate(images, axis=0)
    early = pair_gram(precond, (term,))
    image = (term, partner(2, range(parts)))
    curv = Reduction(1)
    curv.start(early + pair_gram(precond, image[1:]))
    gamma.advance()
    lay(image_ref, image)
    storing[1].start()
    curv.advance()
    gamma.advance()
    curv.advance()
    gamma.advance()
    gamma.finish()
    storing[3].start()
    curv.finish()
    storing[4].start()
    for e in range(3):
        for d in range(4):

            @pl.when(neighbour(d))
            def _():
                for h in range(parts):
                    side_copy(e, h, d, d).wait_send()

    for copy in storing:
        copy.wait()


def update_kernel(*refs):
    inputs, outputs, local = refs[:5], refs[5:7], refs[7:14]
    load_sem, store_sem = refs[14:]
    precond_ref, image_ref, residual_ref, gamma_ref, curv_ref, mult_ref, res_ref = local
    loading = [
        pltpu.make_async_copy(inputs[n], local[n], load_sem.at[n]) for n in range(5)
    ]
    storing = [
        pltpu.make_async_copy(local[5 + n], outputs[n].at[0, 0], store_sem.at[n]) for n in range(2)
    ]
    for copy in loading[::-1]:
        copy.start()
    for copy in loading[3:]:
        copy.wait()
    loads = curv_ref.shape[0]
    width = 8
    matrix = curv_ref[...]
    matrix = 0.5 * (matrix + matrix.T)
    rhs = gamma_ref[...]
    count = loads // width
    left = [matrix[p * width : (p + 1) * width] for p in range(count)]
    right = [rhs[p * width : (p + 1) * width] for p in range(count)]
    shape = (width, loads)
    sub_ids = lax.broadcasted_iota(jnp.int32, shape, 0)

    def column(block, c):
        return jnp.broadcast_to(block[:, c : c + 1], shape)

    def row(block, r):
        return jnp.broadcast_to(block[r : r + 1, :], shape)

    for p in range(count):
        here, there = left[p], right[p]
        cols = [column(here, p * width + j) for j in range(width)]
        for j in range(width):
            inverse = 1.0 / row(cols[j], j)

            def eliminate(block):
                pivot = row(block, j) * inverse
                return jnp.where(sub_ids == j, pivot, block - cols[j] * pivot)

            here, there = eliminate(here), eliminate(there)
            cols = cols[: j + 1] + [eliminate(c) for c in cols[j + 1 :]]
        left[p], right[p] = here, there
        rows_left = [row(here, j) for j in range(width)]
        rows_right = [row(there, j) for j in range(width)]
        order = [(p + k) % count for k in range(1, count)]
        for r in order:
            factors = [column(left[r], p * width + j) for j in range(width)]
            for j in range(width):
                right[r] = right[r] - factors[j] * rows_right[j]
            if p + 1 < count:
                for j in range(width):
                    left[r] = left[r] - factors[j] * rows_left[j]
    alpha = jnp.concatenate(right, axis=0)

    high = alpha.astype(jnp.bfloat16)
    low = (alpha - high.astype(jnp.float32)).astype(jnp.bfloat16)
    parts = jnp.concatenate([high, low], axis=1)
    parts = jnp.concatenate([parts, parts], axis=0)

    def mat_right(pair):
        both = dot(pair, parts)
        return both[:, :loads] + both[:, loads:]

    for copy in loading[:3]:
        copy.wait()
    mult_ref[...] = mat_right(precond_ref[...])
    storing[0].start()
    res_ref[...] = residual_ref[...] - mat_right(image_ref[...])
    storing[1].start()
    for copy in storing:
        copy.wait()


def shards(spans, chords, *args):
    displacement, packed, link_rows = args[0], args[1], args[5]
    size, loads = displacement.shape[2:]
    slots = link_rows.shape[3]
    tile = min(256, size)
    (near, _), *steps = digits(spans)
    fans = sum(radix - 1 for radix, _ in steps)
    group = chords * near
    sems = 2 * (group - 1) + fans
    chunk = loads // group
    f32, bf16 = jnp.float32, jnp.bfloat16
    hbm = pl.BlockSpec(memory_space=pltpu.HBM)
    pair = jax.ShapeDtypeStruct((size, 2 * loads), bf16)
    field = jax.ShapeDtypeStruct((size, loads), f32)
    small = jax.ShapeDtypeStruct((loads, loads), f32)
    middle = pl.pallas_call(
        functools.partial(fields_kernel, spans, chords),
        out_shape=(pair, pair, field, small, small),
        in_specs=[hbm] * 8,
        out_specs=(hbm,) * 5,
        scratch_shapes=[pltpu.VMEM(a.shape, a.dtype) for a in args]
        + [
            pltpu.VMEM((size, size), bf16),
            pltpu.VMEM((size // tile, tile, tile), bf16),
            pltpu.VMEM((size // tile, tile, tile), bf16),
            pltpu.VMEM((3, 2, 4, loads // 2, slots), bf16),
            pltpu.VMEM((3, 2, 4, loads // 2, slots), bf16),
            pltpu.VMEM((2, loads, loads), f32),
            pltpu.VMEM((2, group - 1, chunk, loads), f32),
            pltpu.VMEM((2, len(steps) + 1, chunk, loads), f32),
            pltpu.VMEM((2, max(fans, 1), chunk, loads), f32),
            pltpu.VMEM((2, loads, loads), f32),
            pltpu.SemaphoreType.DMA((3, 2, 4)),
            pltpu.SemaphoreType.DMA((3, 2, 4)),
            pltpu.SemaphoreType.DMA((2, sems)),
            pltpu.SemaphoreType.DMA((2, sems)),
            pltpu.SemaphoreType.DMA((8,)),
            pltpu.VMEM(pair.shape, pair.dtype),
            pltpu.VMEM(pair.shape, pair.dtype),
            pltpu.VMEM(field.shape, field.dtype),
            pltpu.SemaphoreType.DMA((5,)),
        ],
        compiler_params=pltpu.CompilerParams(
            collective_id=0, has_side_effects=True, vmem_limit_bytes=60 * 1024 * 1024
        ),
        name="fields",
    )(*args)
    out = jax.ShapeDtypeStruct((1, 1, size, loads), f32)
    return pl.pallas_call(
        update_kernel,
        out_shape=(out, out),
        in_specs=[hbm] * 5,
        out_specs=(hbm, hbm),
        scratch_shapes=[
            pltpu.VMEM(a.shape, a.dtype) for a in (pair, pair, field, small, small, field, field)
        ]
        + [pltpu.SemaphoreType.DMA((5,)), pltpu.SemaphoreType.DMA((2,))],
        compiler_params=pltpu.CompilerParams(vmem_limit_bytes=60 * 1024 * 1024),
        name="update",
    )(*middle)


def solution(mesh):
    wide = P("span", "chord", None, None)
    narrow = P("span", "chord", None)
    return jax.shard_map(
        functools.partial(shards, mesh.shape["span"], mesh.shape["chord"]),
        mesh=mesh,
        in_specs=(wide, wide, narrow, narrow, narrow, wide, wide, narrow),
        out_specs=(wide, wide),
        check_vma=False,
    )
```

```python
import functools

import jax
import jax.numpy as jnp
from jax import lax
from jax.experimental import pallas as pl
from jax.experimental.pallas import tpu as pltpu
from jax.sharding import PartitionSpec as P

MESH = pl.DeviceIdType.MESH
SIDES = (("span", -1), ("span", 1), ("chord", -1), ("chord", 1))
NT = (((1,), (1,)), ((), ()))


def digits(count):
    out, stride = [], 1
    while count > 1:
        if count % 4 == 0 and out:
            radix = 4
        else:
            radix = next(f for f in range(2, count + 1) if count % f == 0)
        out.append((radix, stride))
        stride *= radix
        count //= radix
    return out


def dot(a, b):
    return jnp.dot(a, b, preferred_element_type=jnp.float32)


def dot_nt(a, b):
    return lax.dot_general(a, b, NT, preferred_element_type=jnp.float32)


def fields_kernel(
    spans,
    chords,
    *refs,
):
    inputs, refs = refs[:8], refs[8:]
    outputs = refs[:5]
    local, refs = refs[5:13], refs[13:]
    disp_ref, packed_ref, fscale_ref, dscale_ref, diag_ref, rows_ref, signs_ref, counts_ref = local
    (
    hot,
    spread,
    mirrors,
    fdiag,
    ddiag,
    sent,
    recv,
    acc,
    scattered,
    held,
    fan,
    full,
    side_send,
    side_recv,
    red_send,
    red_recv,
    load_sem,
    precond_ref,
    image_ref,
    residual_ref,
    store_sem,
    ) = refs
    size, loads = disp_ref.shape[2:]
    slots = rows_ref.shape[3]
    half = sent.shape[3]
    parts = loads // half
    tile = fdiag.shape[1]
    tiles = size // tile
    pos = {"span": lax.axis_index("span"), "chord": lax.axis_index("chord")}
    limit = {"span": spans, "chord": chords}
    (near, _), *steps = digits(spans)
    group = chords * near
    chunk = loads // group

    loading = [
        pltpu.make_async_copy(inputs[n], local[n], load_sem.at[n]) for n in range(8)
    ]
    for n in (5, 0, 6, 7, 1, 3, 4, 2):
        loading[n].start()

    def span_peer(radix, stride, k):
        digit = lax.rem(pos["span"] // stride, radix)
        return pos["span"] + (lax.rem(digit + k, radix) - digit) * stride

    def group_peer(m):
        chord = lax.rem(pos["chord"] + m // near, chords)
        device = {"span": span_peer(near, 1, m % near), "chord": chord}
        return device, chord * near + lax.rem(device["span"], near)

    mine = pl.ds(
        pl.multiple_of((pos["chord"] * near + lax.rem(pos["span"], near)) * chunk, chunk), chunk
    )

    barrier = pltpu.get_barrier_semaphore()
    greeted = [group_peer(m)[0] for m in range(1, group)]
    greeted += [{"span": lax.rem(pos["span"] + k, spans)} for k in (1, spans - 1)]
    greeted += [
        {"span": span_peer(radix, stride, k)} for radix, stride in steps for k in range(1, radix)
    ]
    for device in greeted:
        pl.semaphore_signal(barrier, inc=1, device_id=device, device_id_type=MESH)

    for n in (5, 6, 7):
        loading[n].wait()
    live_signs = []
    for d in range(4):
        rows = rows_ref[0, 0, d : d + 1, :]
        row_ids = lax.broadcasted_iota(jnp.int32, (size, slots), 0)
        hot[:, d * slots : (d + 1) * slots] = jnp.where(row_ids == rows, 1.0, 0.0).astype(
            jnp.bfloat16
        )
        live = lax.broadcasted_iota(jnp.int32, (1, slots), 1) < counts_ref[0, :, d : d + 1]
        live_signs.append(
            jnp.where(live, signs_ref[0, 0, d : d + 1, :], 0).astype(jnp.float32)
        )
    slot_sign = jnp.concatenate(live_signs, axis=1)

    def neighbour(d):
        axis, step = SIDES[d]
        other = pos[axis] + step
        return jnp.logical_and(other >= 0, other < limit[axis])

    def side_copy(e, h, d, slot):
        axis, step = SIDES[d]
        return pltpu.make_async_remote_copy(
            src_ref=sent.at[e, h, d],
            dst_ref=recv.at[e, h, slot],
            send_sem=side_send.at[e, h, d],
            recv_sem=side_recv.at[e, h, slot],
            device_id={axis: pos[axis] + step},
            device_id_type=MESH,
        )

    def send(e, halves, term, scale=None):
        for pair in ((0, 1), (2, 3)):
            here = slice(pair[0] * slots, (pair[1] + 1) * slots)
            values = dot(term, hot[:, here])
            if scale is not None:
                values = values * scale[:, here]
            values = values.astype(jnp.bfloat16)
            for n, h in enumerate(halves):
                for d in pair:
                    sent[e, h, d] = values[
                        n * half : (n + 1) * half,
                        (d - pair[0]) * slots : (d - pair[0] + 1) * slots,
                    ]

                    @pl.when(neighbour(d))
                    def _():
                        side_copy(e, h, d, d ^ 1).start()

    def partner(e, halves):
        total = 0
        for pair in ((2, 3), (0, 1)):
            for d in pair:

                @pl.when(neighbour(d))
                def _():
                    for h in halves:
                        side_copy(e, h, d, d).wait_recv()

            values = [jnp.concatenate([recv[e, h, d] for d in pair], axis=1) for h in halves]
            total += dot(
                jnp.concatenate(values, axis=0), spread[pair[0] * slots : (pair[1] + 1) * slots]
            )
        return total.astype(jnp.bfloat16)

    def apply(diag_blocks, upper, scale, field):
        operand = (scale * sign * field).astype(jnp.bfloat16)
        out = []
        for b in range(tiles):
            lo, hi = b * tile, (b + 1) * tile
            total = dot(operand[:, lo:hi], diag_blocks[b])
            if upper:
                direct, mirrored = (0, lo), (hi, size)
            else:
                direct, mirrored = (hi, size), (0, lo)
            if direct[0] < direct[1]:
                total += dot(
                    operand[:, direct[0] : direct[1]],
                    packed_ref[0, 0, direct[0] : direct[1], lo:hi],
                )
            if mirrored[0] < mirrored[1]:
                total += dot(
                    operand[:, mirrored[0] : mirrored[1]],
                    mirrors[mirrored[0] : mirrored[1], lo:hi],
                )
            out.append(total)
        product = jnp.concatenate(out, axis=1)
        return (sign * scale * product).astype(jnp.bfloat16)

    def pair_gram(left, right):
        return sum(dot_nt(a, b) for a in left for b in right)

    def total_of(pair):
        return pair[0].astype(jnp.float32) + pair[1].astype(jnp.float32)

    class Reduction:
        def __init__(self, g):
            self.g, self.stage = g, 0

        def copy(self, n, src, dst, device):
            return pltpu.make_async_remote_copy(
                src_ref=src,
                dst_ref=dst,
                send_sem=red_send.at[self.g, n],
                recv_sem=red_recv.at[self.g, n],
                device_id=device,
                device_id_type=MESH,
            )

        def copies(self, stage):
            g = self.g
            if stage == 0:
                out = []
                for m in range(1, group):
                    device, owner = group_peer(m)
                    rows = pl.ds(pl.multiple_of(owner * chunk, chunk), chunk)
                    out.append(self.copy(m - 1, acc.at[g, rows], scattered.at[g, m - 1], device))
                return out
            first = group - 1
            fans = [radix - 1 for radix, _ in steps]
            if stage <= len(steps):
                radix, stride = steps[stage - 1]
                base = sum(fans[: stage - 1])
                return [
                    self.copy(
                        first + base + k - 1,
                        held.at[g, stage - 1],
                        fan.at[g, base + k - 1],
                        {"span": span_peer(radix, stride, k)},
                    )
                    for k in range(1, radix)
                ]
            first += sum(fans)
            return [
                self.copy(
                    first + m - 1, held.at[g, len(steps)], full.at[g, mine], group_peer(m)[0]
                )
                for m in range(1, group)
            ]

        def start(self, value):
            acc[self.g] = value
            for copy in self.copies(0):
                copy.start()

        def advance(self):
            if self.stage > len(steps) + 1:
                return
            g, stage = self.g, self.stage
            copies = self.copies(stage)
            for copy in copies:
                copy.wait_recv()
            if stage == 0:
                total = acc[g, mine]
                for m in range(1, group):
                    total += scattered[g, m - 1]
            elif stage <= len(steps):
                base = sum(radix - 1 for radix, _ in steps[: stage - 1])
                total = held[g, stage - 1]
                for k in range(steps[stage - 1][0] - 1):
                    total += fan[g, base + k]
            if stage <= len(steps):
                held[g, stage] = total
                if stage == len(steps):
                    full[g, mine] = total
                for copy in self.copies(stage + 1):
                    copy.start()
            self.stage += 1

        def finish(self):
            while self.stage <= len(steps) + 1:
                self.advance()
            for stage in range(len(steps) + 2):
                for copy in self.copies(stage):
                    copy.wait_send()

    def lay(ref, pair):
        for n, part in enumerate(pair):
            ref[:, n * loads : (n + 1) * loads] = part.astype(jnp.float32).T.astype(ref.dtype)

    stored = (precond_ref, image_ref, residual_ref, full.at[0], full.at[1])
    storing = [
        pltpu.make_async_copy(stored[n], outputs[n], store_sem.at[n]) for n in range(5)
    ]

    loading[0].wait()
    disp = disp_ref[0, 0].astype(jnp.float32).T
    for d in range(4):

        @pl.when(jnp.logical_not(neighbour(d)))
        def _():
            for e in range(3):
                for h in range(parts):
                    recv[e, h, d] = jnp.zeros(recv.shape[3:], recv.dtype)

    pl.semaphore_wait(barrier, len(greeted))
    send(0, range(parts), disp.astype(jnp.bfloat16), slot_sign)
    for d in range(4):
        rows = jnp.broadcast_to(rows_ref[0, 0, d : d + 1, :], (8, slots)).astype(jnp.float32)
        rows = rows.T.astype(jnp.int32)[:, 0:1]
        row_ids = lax.broadcasted_iota(jnp.int32, (slots, size), 1)
        spread[d * slots : (d + 1) * slots] = jnp.where(row_ids == rows, 1.0, 0.0).astype(
            jnp.bfloat16
        )
    signs = jnp.broadcast_to(slot_sign, (16, size)).astype(jnp.bfloat16)
    sign = dot(signs, spread[...])[0:1, :]
    gap = (sign * disp).astype(jnp.bfloat16)
    for n in (1, 2, 3, 4):
        loading[n].wait()
    for b in range(tiles):
        lo, hi = b * tile, (b + 1) * tile
        here = packed_ref[0, 0, lo:hi, lo:hi].astype(jnp.float32)
        mirror = here.T
        row_ids = lax.broadcasted_iota(jnp.int32, (tile, tile), 0)
        col_ids = lax.broadcasted_iota(jnp.int32, (tile, tile), 1)
        fdiag[b] = jnp.where(col_ids >= row_ids, here, mirror).astype(jnp.bfloat16)
        lower = jnp.where(row_ids > col_ids, here, mirror)
        diag = diag_ref[0, :, lo:hi].astype(jnp.float32)
        ddiag[b] = jnp.where(row_ids == col_ids, diag, lower).astype(jnp.bfloat16)

    def mirror_blocks(upper):
        for b in range(tiles):
            for a in range(b + 1, tiles) if upper else range(b):
                ra, rb = slice(a * tile, (a + 1) * tile), slice(b * tile, (b + 1) * tile)
                mirrors[ra, rb] = packed_ref[0, 0, rb, ra].T

    mirror_blocks(False)
    fscale = fscale_ref[0]
    dscale = dscale_ref[0]

    def rows_of(pieces):
        return tuple(jnp.concatenate([p[n] for p in pieces], axis=0) for n in range(2))

    right, terms = [], []
    for h in range(parts):
        right.append((gap[h * half : (h + 1) * half], partner(0, (h,))))
        terms.append(apply(ddiag, False, dscale, total_of(right[h])))
        send(1, (h,), terms[h])
    right = rows_of(right)
    residual_ref[...] = total_of(right).T
    storing[2].start()
    mirror_blocks(True)
    precond, images = [], []
    for h in range(parts):
        precond.append((terms[h], partner(1, (h,))))
        images.append(apply(fdiag, True, fscale, total_of(precond[h])))
        send(2, (h,), images[h])
    precond = rows_of(precond)
    gamma = Reduction(0)
    gamma.start(pair_gram(precond, right))
    lay(precond_ref, precond)
    storing[0].start()
    term = jnp.concatenate(images, axis=0)
    early = pair_gram(precond, (term,))
    image = (term, partner(2, range(parts)))
    curv = Reduction(1)
    curv.start(early + pair_gram(precond, image[1:]))
    gamma.advance()
    lay(image_ref, image)
    storing[1].start()
    curv.advance()
    gamma.advance()
    curv.advance()
    gamma.advance()
    gamma.finish()
    storing[3].start()
    curv.finish()
    storing[4].start()
    for e in range(3):
        for d in range(4):

            @pl.when(neighbour(d))
            def _():
                for h in range(parts):
                    side_copy(e, h, d, d).wait_send()

    for copy in storing:
        copy.wait()


def update_kernel(*refs):
    inputs, outputs, local = refs[:5], refs[5:7], refs[7:14]
    load_sem, store_sem = refs[14:]
    precond_ref, image_ref, residual_ref, gamma_ref, curv_ref, mult_ref, res_ref = local
    loading = [
        pltpu.make_async_copy(inputs[n], local[n], load_sem.at[n]) for n in range(5)
    ]
    storing = [
        pltpu.make_async_copy(local[5 + n], outputs[n].at[0, 0], store_sem.at[n]) for n in range(2)
    ]
    for copy in loading[::-1]:
        copy.start()
    for copy in loading[3:]:
        copy.wait()
    loads = curv_ref.shape[0]
    width = 8
    matrix = curv_ref[...]
    matrix = 0.5 * (matrix + matrix.T)
    rhs = gamma_ref[...]
    count = loads // width
    left = [matrix[p * width : (p + 1) * width] for p in range(count)]
    right = [rhs[p * width : (p + 1) * width] for p in range(count)]
    shape = (width, loads)
    sub_ids = lax.broadcasted_iota(jnp.int32, shape, 0)

    def column(block, c):
        return jnp.broadcast_to(block[:, c : c + 1], shape)

    def row(block, r):
        return jnp.broadcast_to(block[r : r + 1, :], shape)

    for p in range(count):
        here, there = left[p], right[p]
        cols = [column(here, p * width + j) for j in range(width)]
        for j in range(width):
            inverse = 1.0 / row(cols[j], j)

            def eliminate(block):
                pivot = row(block, j) * inverse
                return jnp.where(sub_ids == j, pivot, block - cols[j] * pivot)

            here, there = eliminate(here), eliminate(there)
            cols = cols[: j + 1] + [eliminate(c) for c in cols[j + 1 :]]
        left[p], right[p] = here, there
        rows_left = [row(here, j) for j in range(width)]
        rows_right = [row(there, j) for j in range(width)]
        order = [(p + k) % count for k in range(1, count)]
        for r in order:
            factors = [column(left[r], p * width + j) for j in range(width)]
            for j in range(width):
                right[r] = right[r] - factors[j] * rows_right[j]
            if p + 1 < count:
                for j in range(width):
                    left[r] = left[r] - factors[j] * rows_left[j]
    alpha = jnp.concatenate(right, axis=0)

    high = alpha.astype(jnp.bfloat16)
    low = (alpha - high.astype(jnp.float32)).astype(jnp.bfloat16)
    parts = jnp.concatenate([high, low], axis=1)
    parts = jnp.concatenate([parts, parts], axis=0)

    def mat_right(pair):
        both = dot(pair, parts)
        return both[:, :loads] + both[:, loads:]

    for copy in loading[:3]:
        copy.wait()
    mult_ref[...] = mat_right(precond_ref[...])
    storing[0].start()
    res_ref[...] = residual_ref[...] - mat_right(image_ref[...])
    storing[1].start()
    for copy in storing:
        copy.wait()


def shards(spans, chords, *args):
    displacement, packed, link_rows = args[0], args[1], args[5]
    size, loads = displacement.shape[2:]
    slots = link_rows.shape[3]
    tile = min(256, size)
    (near, _), *steps = digits(spans)
    fans = sum(radix - 1 for radix, _ in steps)
    group = chords * near
    sems = 2 * (group - 1) + fans
    chunk = loads // group
    f32, bf16 = jnp.float32, jnp.bfloat16
    hbm = pl.BlockSpec(memory_space=pltpu.HBM)
    pair = jax.ShapeDtypeStruct((size, 2 * loads), bf16)
    field = jax.ShapeDtypeStruct((size, loads), f32)
    small = jax.ShapeDtypeStruct((loads, loads), f32)
    middle = pl.pallas_call(
        functools.partial(fields_kernel, spans, chords),
        out_shape=(pair, pair, field, small, small),
        in_specs=[hbm] * 8,
        out_specs=(hbm,) * 5,
        scratch_shapes=[pltpu.VMEM(a.shape, a.dtype) for a in args]
        + [
            pltpu.VMEM((size, size), bf16),
            pltpu.VMEM((size, size), bf16),
            pltpu.VMEM((size, size), bf16),
            pltpu.VMEM((size // tile, tile, tile), bf16),
            pltpu.VMEM((size // tile, tile, tile), bf16),
            pltpu.VMEM((3, 2, 4, loads // 2, slots), bf16),
            pltpu.VMEM((3, 2, 4, loads // 2, slots), bf16),
            pltpu.VMEM((2, loads, loads), f32),
            pltpu.VMEM((2, group - 1, chunk, loads), f32),
            pltpu.VMEM((2, len(steps) + 1, chunk, loads), f32),
            pltpu.VMEM((2, max(fans, 1), chunk, loads), f32),
            pltpu.VMEM((2, loads, loads), f32),
            pltpu.SemaphoreType.DMA((3, 2, 4)),
            pltpu.SemaphoreType.DMA((3, 2, 4)),
            pltpu.SemaphoreType.DMA((2, sems)),
            pltpu.SemaphoreType.DMA((2, sems)),
            pltpu.SemaphoreType.DMA((8,)),
            pltpu.VMEM(pair.shape, pair.dtype),
            pltpu.VMEM(pair.shape, pair.dtype),
            pltpu.VMEM(field.shape, field.dtype),
            pltpu.SemaphoreType.DMA((5,)),
        ],
        compiler_params=pltpu.CompilerParams(
            collective_id=0, has_side_effects=True, vmem_limit_bytes=60 * 1024 * 1024
        ),
        name="fields",
    )(*args)
    out = jax.ShapeDtypeStruct((1, 1, size, loads), f32)
    return pl.pallas_call(
        update_kernel,
        out_shape=(out, out),
        in_specs=[hbm] * 5,
        out_specs=(hbm, hbm),
        scratch_shapes=[
            pltpu.VMEM(a.shape, a.dtype) for a in (pair, pair, field, small, small, field, field)
        ]
        + [pltpu.SemaphoreType.DMA((5,)), pltpu.SemaphoreType.DMA((2,))],
        compiler_params=pltpu.CompilerParams(vmem_limit_bytes=60 * 1024 * 1024),
        name="update",
    )(*middle)


def solution(mesh):
    wide = P("span", "chord", None, None)
    narrow = P("span", "chord", None)
    return jax.shard_map(
        functools.partial(shards, mesh.shape["span"], mesh.shape["chord"]),
        mesh=mesh,
        in_specs=(wide, wide, narrow, narrow, narrow, wide, wide, narrow),
        out_specs=(wide, wide),
        check_vma=False,
    )
```
